32 devices in a mesh: grp: 2 (over y), rec: 4 (over z), smp: 4 (over x, core).
Axes of the slice: x: 2, y: 2, z: 4, core: 2. Of those that a mesh axis runs over, the one named last changes fastest.
Arguments:
- records: bfloat16 [2048, 16384], P(('grp', 'rec'), 'smp'), parts along dimension 0, may hold values from -24 to 24
- start_modes: float32 [4, 8192, 128], P('smp', ('grp', 'rec')), parts along dimension 1, may hold values from -6 to 6
Outputs:
- covariance: float32 [4, 8192, 16384], P(None, ('grp', 'rec'), 'smp'), parts along dimension 1
- modes: float32 [4, 8192, 128], P('smp', ('grp', 'rec')), parts along dimension 1
- projections: float32 [2048, 128], P(('grp', 'rec')), parts along dimension 0
The draws below stay inside these ranges and needn't reach their ends.
There are 2 independent parts, one for each index of `grp`. The reference program is written for one: setup_inputs(seed, part) draws one part's arguments, and reference() takes and returns one part's arrays. A program takes and returns all parts, laid end to end along the dimension named above; each array names one. Nothing has to cross between parts.
All inputs are finite; a program needn't handle non-finite values.
Results may differ from the reference program's by a relative error of at most 0.0003.
Values may be sent and summed in bfloat16 or wider, within the bound.
A program may use at most 192 MiB of HBM per device.

```python
import math
import jax
import jax.numpy as jnp
from jax import lax

S = 16384
K = 128
RECORDS = 1024
ITERS = 2
SUB = 1024
N_REC = 4
N_SMP = 4


def block_scales(key):
    blocks = N_SMP * N_REC
    drawn = jnp.exp(jax.random.uniform(jax.random.fold_in(key, 11), (blocks,), jnp.float32, 0.0, 0.693))
    chosen = jax.random.randint(jax.random.fold_in(key, 12), (), 0, blocks)
    scales = jnp.where(jnp.arange(blocks) == chosen, 4.0, drawn)
    sample = jnp.arange(S)
    outer = sample // (S // N_SMP)
    inner = sample % (S // N_SMP) // SUB
    return scales[outer * N_REC + inner]


def draw_records(key, part):
    key = jax.random.fold_in(key, 5)
    scale = block_scales(key)
    base = jnp.clip(jax.random.normal(jax.random.fold_in(key, 21), (RECORDS, S), jnp.float32), -6.0, 6.0)
    return (base * scale[None, :]).astype(jnp.bfloat16)


def block_levels(stream_key, shape, shards, least, largest):
    factor_of = 1.0
    for axis_at, blocks in shards:
        heights = jax.random.uniform(jax.random.fold_in(jax.random.fold_in(stream_key, 6), axis_at), (blocks,), jnp.float32, least / len(shards), largest / len(shards))
        factor_of = factor_of * jnp.repeat(jnp.exp(heights), shape[axis_at] // blocks).reshape((-1,) + (1,) * (len(shape) - 1 - axis_at))
    return factor_of


def noise(key, dims, deviation, limit, shards=(), held_as=jnp.bfloat16):
    entries = jax.random.normal(key, dims, jnp.float32) * deviation
    if len(shards) > 0:
        entries = block_levels(key, dims, shards, -0.22, 0.18) * entries
    return jnp.clip(entries, min=-limit, max=limit).astype(held_as)


def setup_inputs(seed: int = 0, part: int = 0) -> dict:
    keys = jax.random.split(jax.random.key(seed), 3)
    part_splits = jax.random.split(jax.random.fold_in(keys[2], part), 3)
    return {
        "records": draw_records(jax.random.fold_in(jax.random.fold_in(keys[2], part), 71), part),
        "start_modes": noise(part_splits[1], (N_SMP, S // N_SMP, K), 1.0, 6.0, ((0, 4), (1, 4)), jnp.float32),
    }


def orthonormal(block):
    inner = jnp.dot(block.T, block, precision=lax.Precision.HIGHEST)
    factor = jnp.linalg.cholesky(inner)
    return lax.linalg.triangular_solve(factor, block, left_side=False, lower=True, transpose_a=True)

def reference(records, start_modes):
    covar = jnp.dot(records.T.astype(jnp.float32), records.astype(jnp.float32), preferred_element_type=jnp.float32) / RECORDS
    subspace = start_modes.reshape(S, K)
    for step in range(ITERS):
        subspace = jnp.dot(covar, subspace, precision=lax.Precision.HIGHEST)
    subspace = orthonormal(subspace)
    amplitude = jnp.dot(records.astype(jnp.float32), subspace, precision=lax.Precision.HIGHEST) / math.sqrt(S)
    covariance = covar.reshape(N_SMP, S // N_SMP, S)
    modes = (subspace * math.sqrt(S)).reshape(N_SMP, S // N_SMP, K)
    return (covariance, modes, amplitude)
```

```python
import math

import jax
import jax.numpy as jnp
from jax import lax
from jax.sharding import PartitionSpec as P

HIGHEST = lax.Precision.HIGHEST


def pieces(block):
    parts = []
    for _ in range(2):
        high = lax.reduce_precision(block, 8, 7)
        parts.append(high.astype(jnp.bfloat16))
        block = block - high
    parts.append(block.astype(jnp.bfloat16))
    return jnp.concatenate(parts, axis=1)


def exact_dot(left, block, contract):
    kept = block.shape[1]
    out = lax.dot_general(
        left, pieces(block), (((contract,), (0,)), ((), ())), preferred_element_type=jnp.float32
    )
    return out[:, :kept] + out[:, kept : 2 * kept] + out[:, 2 * kept :]


def on_device(records, start_modes):
    rec_dev, width = records.shape
    panels = lax.axis_size("smp")
    total = rec_dev * lax.axis_size("rec")
    sub_width, kept = start_modes.shape[1:]
    full_width = width * panels
    at = lax.axis_index("rec")

    block = lax.all_gather(records, "rec", axis=0, tiled=True)
    own = lax.dynamic_slice_in_dim(block, at * sub_width, sub_width, axis=1)
    row_block = lax.all_gather(own, "smp", axis=1, tiled=True)

    gram = lax.psum(
        lax.dot_general(
            records, block, (((1,), (1,)), ((), ())), preferred_element_type=jnp.float32
        ),
        "smp",
    ) / total
    first = lax.psum(exact_dot(own, start_modes[0], 1), ("rec", "smp"))
    second_own = jnp.dot(gram, first, precision=HIGHEST)
    second = lax.all_gather(second_own, "rec", axis=0, tiled=True)
    amplitude = jnp.dot(gram, second, precision=HIGHEST)
    inner = lax.psum(jnp.dot(second_own.T, amplitude, precision=HIGHEST), "rec") / total

    tile = (
        lax.dot_general(
            row_block, block, (((0,), (0,)), ((), ())), preferred_element_type=jnp.float32
        )
        / total
    )
    covariance = tile.reshape(panels, sub_width, width)

    factor = jnp.linalg.cholesky(inner)
    solved = lax.linalg.triangular_solve(
        factor,
        jnp.concatenate([second, amplitude], axis=0),
        left_side=False,
        lower=True,
        transpose_a=True,
    )
    modes = exact_dot(own, solved[:total], 0) * (math.sqrt(full_width) / total)
    projections = solved[total:] / math.sqrt(full_width)
    return (covariance, modes.reshape(1, sub_width, kept), projections)


def solution(mesh):
    in_specs = (P(("grp", "rec"), "smp"), P("smp", ("grp", "rec"), None))
    out_specs = (
        P(None, ("grp", "rec"), "smp"),
        P("smp", ("grp", "rec"), None),
        P(("grp", "rec"), None),
    )
    return jax.shard_map(
        on_device, mesh=mesh, in_specs=in_specs, out_specs=out_specs, check_vma=False
    )
```

```python
import functools
import math

import jax
import jax.numpy as jnp
from jax import lax
from jax.experimental import pallas as pl
from jax.experimental.pallas import tpu as pltpu
from jax.sharding import PartitionSpec as P

HIGHEST = lax.Precision.HIGHEST


def remote(src, dst, send_sem, recv_sem, device):
    return pltpu.make_async_remote_copy(
        src_ref=src,
        dst_ref=dst,
        send_sem=send_sem,
        recv_sem=recv_sem,
        device_id=device,
        device_id_type=pl.DeviceIdType.MESH,
    )


def greet(devices):
    barrier = pltpu.get_barrier_semaphore()
    for device in devices:
        pl.semaphore_signal(barrier, inc=1, device_id=device, device_id_type=pl.DeviceIdType.MESH)
    pl.semaphore_wait(barrier, len(devices))


def gather_kernel(n, m, rec_ref, block_ref, row_ref, up_sem, down_sem, in_sem, out_x, in_x, local):
    g, r, s = lax.axis_index("grp"), lax.axis_index("rec"), lax.axis_index("smp")
    rows, width = rec_ref.shape
    sub = width // n
    up, down = lax.rem(r + 1, n), lax.rem(r + n - 1, n)
    across = [lax.rem(s + k, m) for k in range(1, m)]
    greet([(g, up, s), (g, down, s)] + [(g, r, d) for d in across])

    def spot(ref, b, q):
        return ref.at[pl.ds(pl.multiple_of(b * rows, rows), rows), pl.ds(pl.multiple_of(q * sub, sub), sub)]

    def chunk(b, q, own):
        return rec_ref.at[:, pl.ds(q * sub, sub)] if own else spot(block_ref, b, q)

    def send_up(b, q, own):
        return remote(chunk(b, q, own), spot(block_ref, b, q), up_sem.at[b, q], in_sem.at[b, q], (g, up, s))

    def send_down(b, q, own):
        return remote(chunk(b, q, own), spot(block_ref, b, q), down_sem.at[b, q], in_sem.at[b, q], (g, down, s))

    def mine(b, own):
        if own:
            return rec_ref.at[:, pl.ds(pl.multiple_of(r * sub, sub), sub)]
        return spot(block_ref, b, r)

    def send_across(b, k, own):
        return remote(mine(b, own), spot(row_ref, b, s), out_x.at[k, b], in_x.at[k, b], (g, r, across[k]))

    def keep(b, own):
        return pltpu.make_async_copy(mine(b, own), spot(row_ref, b, s), local.at[b])

    def spread(b, own):
        for k in range(m - 1):
            send_across(b, k, own).start()
        keep(b, own).start()

    whole = pltpu.make_async_copy(
        rec_ref, block_ref.at[pl.ds(pl.multiple_of(r * rows, rows), rows)], local.at[n]
    )
    for i in range(n):
        @pl.when(r < n - 1)
        def _():
            send_up(r, n - 1 - i, True).start()

        @pl.when(r > 0)
        def _():
            send_down(r, i, True).start()

    spread(r, True)
    whole.start()
    for t in range(1, n):
        for i in range(n):
            @pl.when(r + t < n)
            def _():
                b, q = r + t, i
                send_down(b, q, False).wait_recv()

                @pl.when(r > 0)
                def _():
                    send_down(b, q, False).start()

                @pl.when(r == q)
                def _():
                    spread(b, False)

            @pl.when(r - t >= 0)
            def _():
                b, q = r - t, n - 1 - i
                send_up(b, q, False).wait_recv()

                @pl.when(r < n - 1)
                def _():
                    send_up(b, q, False).start()

                @pl.when(r == q)
                def _():
                    spread(b, False)

    whole.wait()
    for i in range(n):
        @pl.when(r < n - 1)
        def _():
            send_up(r, i, True).wait_send()

        @pl.when(r > 0)
        def _():
            send_down(r, i, True).wait_send()

        for t in range(1, n):
            @pl.when((r + t < n) & (r > 0))
            def _():
                send_down(r + t, i, False).wait_send()

            @pl.when((r - t >= 0) & (r < n - 1))
            def _():
                send_up(r - t, i, False).wait_send()

    for b in range(n):
        pltpu.make_async_copy(spot(block_ref, b, r), spot(row_ref, b, s), local.at[b]).wait()
        for k in range(m - 1):
            copy = remote(
                spot(block_ref, b, r), spot(row_ref, b, lax.rem(s + m - 1 - k, m)),
                out_x.at[k, b], in_x.at[k, b], (g, r, across[k]),
            )
            copy.wait_send()
            copy.wait_recv()


def gather(records, n, m):
    rows, width = records.shape
    full = jax.ShapeDtypeStruct((rows * n, width), records.dtype)
    wide = jax.ShapeDtypeStruct((rows * n, width // n * m), records.dtype)
    dma = pltpu.SemaphoreType.DMA
    return pl.pallas_call(
        functools.partial(gather_kernel, n, m),
        out_shape=(full, wide),
        in_specs=[pl.BlockSpec(memory_space=pl.ANY)],
        out_specs=(pl.BlockSpec(memory_space=pl.ANY), pl.BlockSpec(memory_space=pl.ANY)),
        scratch_shapes=[
            dma((n, n)), dma((n, n)), dma((n, n)), dma((m - 1, n)), dma((m - 1, n)), dma((n + 1,)),
        ],
        compiler_params=pltpu.CompilerParams(collective_id=0, has_side_effects=True),
        name="gather_records",
    )(records)


def iterate_kernel(
    total, x_ref, w_ref, t_ref, c_ref,
    pair_in, cross_out, cross_in, z_out, z_in, w_out, w_in, t_out, t_in, c_out, c_in,
    send_sem, recv_sem,
):
    g, r, s = lax.axis_index("grp"), lax.axis_index("rec"), lax.axis_index("smp")

    def flip(a, bit):
        return a + bit - 2 * bit * lax.rem(a // bit, 2)

    r1, r2 = flip(r, 1), flip(r, 2)
    s1, s2 = flip(s, 1), flip(s, 2)
    r3 = flip(r2, 1)
    greet([(g, r1, s), (g, r2, s), (g, r3, s), (g, r, s1), (g, r, s2)])
    kept = w_ref.shape[2]

    def swap(at, src, dst, device):
        return remote(src, dst, send_sem.at[at], recv_sem.at[at], device)

    first = swap(0, x_ref.at[s1], pair_in.at[0], (g, r, s1))
    second = swap(1, x_ref.at[flip(s2, 1)], pair_in.at[1], (g, r, s1))
    second.start()
    first.start()
    second.wait()
    cross_out[...] = x_ref[s2] + pair_in[1]
    cross = swap(2, cross_out, cross_in, (g, r, s2))
    cross.start()
    first.wait()
    cross.wait()
    strip = x_ref[s] + pair_in[0] + cross_in[...]
    size = strip.shape[1] - kept
    gram = strip[:, :size].T / total

    def add_up(at, value, outs, ins, devices):
        for i, device in enumerate(devices):
            outs[i] = value
            copy = swap(at + i, outs.at[i], ins.at[i], device)
            copy.start()
            copy.wait()
            value = value + ins[i]
        return value

    rec_pair = [(g, r1, s), (g, r2, s)]
    smp_pair = [(g, r, s1), (g, r, s2)]
    start = add_up(3, strip[:, size:], z_out, z_in, rec_pair)
    own = add_up(5, jnp.dot(gram, start, precision=HIGHEST), w_out, w_in, smp_pair)
    w_ref[r] = own
    copies = [
        swap(7 + i, w_ref.at[r], w_ref.at[r], (g, d, s)) for i, d in enumerate((r1, r2, r3))
    ]
    for copy in copies:
        copy.start()
    for i, d in enumerate((r1, r2, r3)):
        swap(7 + i, w_ref.at[d], w_ref.at[d], (g, d, s)).wait_recv()
    amplitude = add_up(10, jnp.dot(gram, w_ref[s], precision=HIGHEST), t_out, t_in, smp_pair)
    t_ref[...] = amplitude
    inner = jnp.dot(own.T, amplitude, precision=HIGHEST) / total
    c_ref[...] = add_up(12, inner, c_out, c_in, rec_pair)
    for copy in copies:
        copy.wait_send()


def iterate(x, kept, n, m):
    total, width = x.shape
    rows = total // n
    f32 = jnp.float32
    vmem = pl.BlockSpec(memory_space=pltpu.VMEM)
    pair = pltpu.VMEM((2, rows, kept), f32)
    inner = pltpu.VMEM((2, kept, kept), f32)
    w, t, c = pl.pallas_call(
        functools.partial(iterate_kernel, total),
        out_shape=(
            jax.ShapeDtypeStruct((n, rows, kept), f32),
            jax.ShapeDtypeStruct((rows, kept), f32),
            jax.ShapeDtypeStruct((kept, kept), f32),
        ),
        in_specs=[vmem],
        out_specs=(vmem, vmem, vmem),
        scratch_shapes=[
            pltpu.VMEM((2, rows, width), f32),
            pltpu.VMEM((rows, width), f32),
            pltpu.VMEM((rows, width), f32),
            pair, pair, pair, pair, pair, pair, inner, inner,
            pltpu.SemaphoreType.DMA((14,)),
            pltpu.SemaphoreType.DMA((14,)),
        ],
        compiler_params=pltpu.CompilerParams(
            collective_id=1, has_side_effects=True, vmem_limit_bytes=32 * 2**20
        ),
        name="iterate_modes",
    )(x.reshape(m, rows, width))
    return w.reshape(total, kept), t, c


def pieces(block):
    parts = []
    for _ in range(2):
        high = lax.reduce_precision(block, 8, 7)
        parts.append(high.astype(jnp.bfloat16))
        block = block - high
    parts.append(block.astype(jnp.bfloat16))
    return jnp.concatenate(parts, axis=1)


def exact_dot(left, block, contract):
    kept = block.shape[1]
    out = lax.dot_general(
        left, pieces(block), (((contract,), (0,)), ((), ())), preferred_element_type=jnp.float32
    )
    return out[:, :kept] + out[:, kept : 2 * kept] + out[:, 2 * kept :]


def on_device(records, start_modes):
    rec_dev, width = records.shape
    panels = lax.axis_size("smp")
    total = rec_dev * lax.axis_size("rec")
    sub_width, kept = start_modes.shape[1:]
    full_width = width * panels
    at = lax.axis_index("rec")

    n, m = lax.axis_size("rec"), panels
    direct = n == 4 and m == 4 and sub_width % 128 == 0 and rec_dev % 128 == 0 and kept % 128 == 0
    if direct:
        block, row_block = gather(records, n, m)
    else:
        block = lax.all_gather(records, "rec", axis=0, tiled=True)
    own = lax.dynamic_slice_in_dim(block, at * sub_width, sub_width, axis=1)
    if not direct:
        row_block = lax.all_gather(own, "smp", axis=1, tiled=True)

    gram_part = lax.dot_general(
        block, records, (((1,), (1,)), ((), ())), preferred_element_type=jnp.float32
    )
    first_part = exact_dot(own, start_modes[0], 1)
    if direct:
        stacked = jnp.concatenate([gram_part, first_part], axis=1)
        second, amplitude, inner = iterate(stacked, kept, n, m)
    else:
        gram = lax.psum(gram_part, "smp").T / total
        first = lax.psum(first_part, ("rec", "smp"))
        second_own = jnp.dot(gram, first, precision=HIGHEST)
        second = lax.all_gather(second_own, "rec", axis=0, tiled=True)
        amplitude = jnp.dot(gram, second, precision=HIGHEST)
        inner = lax.psum(jnp.dot(second_own.T, amplitude, precision=HIGHEST), "rec") / total

    tile = (
        lax.dot_general(
            row_block, block, (((0,), (0,)), ((), ())), preferred_element_type=jnp.float32
        )
        / total
    )
    covariance = tile.reshape(panels, sub_width, width)

    factor = jnp.linalg.cholesky(inner)
    solved = lax.linalg.triangular_solve(
        factor,
        jnp.concatenate([second, amplitude], axis=0),
        left_side=False,
        lower=True,
        transpose_a=True,
    )
    modes = exact_dot(own, solved[:total], 0) * (math.sqrt(full_width) / total)
    projections = solved[total:] / math.sqrt(full_width)
    return (covariance, modes.reshape(1, sub_width, kept), projections)


def solution(mesh):
    in_specs = (P(("grp", "rec"), "smp"), P("smp", ("grp", "rec"), None))
    out_specs = (
        P(None, ("grp", "rec"), "smp"),
        P("smp", ("grp", "rec"), None),
        P(("grp", "rec"), None),
    )
    return jax.shard_map(
        on_device, mesh=mesh, in_specs=in_specs, out_specs=out_specs, check_vma=False
    )
```

```python
import functools
import math

import jax
import jax.numpy as jnp
from jax import lax
from jax.experimental import pallas as pl
from jax.experimental.pallas import tpu as pltpu
from jax.sharding import PartitionSpec as P

HIGHEST = lax.Precision.HIGHEST


def remote(src, dst, send_sem, recv_sem, device):
    return pltpu.make_async_remote_copy(
        src_ref=src,
        dst_ref=dst,
        send_sem=send_sem,
        recv_sem=recv_sem,
        device_id=device,
        device_id_type=pl.DeviceIdType.MESH,
    )


def greet(devices):
    barrier = pltpu.get_barrier_semaphore()
    for device in devices:
        pl.semaphore_signal(barrier, inc=1, device_id=device, device_id_type=pl.DeviceIdType.MESH)
    pl.semaphore_wait(barrier, len(devices))


def gather_kernel(n, m, rec_ref, block_ref, row_ref, up_sem, down_sem, in_sem, out_x, in_x, local):
    g, r, s = lax.axis_index("grp"), lax.axis_index("rec"), lax.axis_index("smp")
    rows, width = rec_ref.shape
    sub = width // n
    up, down = lax.rem(r + 1, n), lax.rem(r + n - 1, n)
    across = [lax.rem(s + k, m) for k in range(1, m)]
    greet([(g, up, s), (g, down, s)] + [(g, r, d) for d in across])

    def spot(ref, b, q):
        return ref.at[pl.ds(pl.multiple_of(b * rows, rows), rows), pl.ds(pl.multiple_of(q * sub, sub), sub)]

    def chunk(b, q, own):
        return rec_ref.at[:, pl.ds(q * sub, sub)] if own else spot(block_ref, b, q)

    def send_up(b, q, own):
        return remote(chunk(b, q, own), spot(block_ref, b, q), up_sem.at[b, q], in_sem.at[b, q], (g, up, s))

    def send_down(b, q, own):
        return remote(chunk(b, q, own), spot(block_ref, b, q), down_sem.at[b, q], in_sem.at[b, q], (g, down, s))

    def mine(b, own):
        if own:
            return rec_ref.at[:, pl.ds(pl.multiple_of(r * sub, sub), sub)]
        return spot(block_ref, b, r)

    def send_across(b, k, own):
        return remote(mine(b, own), spot(row_ref, b, s), out_x.at[k, b], in_x.at[k, b], (g, r, across[k]))

    def keep(b, own):
        return pltpu.make_async_copy(mine(b, own), spot(row_ref, b, s), local.at[b])

    def spread(b, own):
        for k in range(m - 1):
            send_across(b, k, own).start()
        keep(b, own).start()

    whole = pltpu.make_async_copy(
        rec_ref, block_ref.at[pl.ds(pl.multiple_of(r * rows, rows), rows)], local.at[n]
    )
    for i in range(n):
        @pl.when(r < n - 1)
        def _():
            send_up(r, n - 1 - i, True).start()

        @pl.when(r > 0)
        def _():
            send_down(r, i, True).start()

    spread(r, True)
    whole.start()
    for t in range(1, n):
        for i in range(n):
            @pl.when(r + t < n)
            def _():
                b, q = r + t, i
                send_down(b, q, False).wait_recv()

                @pl.when(r > 0)
                def _():
                    send_down(b, q, False).start()

                @pl.when(r == q)
                def _():
                    spread(b, False)

            @pl.when(r - t >= 0)
            def _():
                b, q = r - t, n - 1 - i
                send_up(b, q, False).wait_recv()

                @pl.when(r < n - 1)
                def _():
                    send_up(b, q, False).start()

                @pl.when(r == q)
                def _():
                    spread(b, False)

    whole.wait()
    for i in range(n):
        @pl.when(r < n - 1)
        def _():
            send_up(r, i, True).wait_send()

        @pl.when(r > 0)
        def _():
            send_down(r, i, True).wait_send()

        for t in range(1, n):
            @pl.when((r + t < n) & (r > 0))
            def _():
                send_down(r + t, i, False).wait_send()

            @pl.when((r - t >= 0) & (r < n - 1))
            def _():
                send_up(r - t, i, False).wait_send()

    for b in range(n):
        pltpu.make_async_copy(spot(block_ref, b, r), spot(row_ref, b, s), local.at[b]).wait()
        for k in range(m - 1):
            copy = remote(
                spot(block_ref, b, r), spot(row_ref, b, lax.rem(s + m - 1 - k, m)),
                out_x.at[k, b], in_x.at[k, b], (g, r, across[k]),
            )
            copy.wait_send()
            copy.wait_recv()


def gather(records, n, m):
    rows, width = records.shape
    full = jax.ShapeDtypeStruct((rows * n, width), records.dtype)
    wide = jax.ShapeDtypeStruct((rows * n, width // n * m), records.dtype)
    dma = pltpu.SemaphoreType.DMA
    return pl.pallas_call(
        functools.partial(gather_kernel, n, m),
        out_shape=(full, wide),
        in_specs=[pl.BlockSpec(memory_space=pl.ANY)],
        out_specs=(pl.BlockSpec(memory_space=pl.ANY), pl.BlockSpec(memory_space=pl.ANY)),
        scratch_shapes=[
            dma((n, n)), dma((n, n)), dma((n, n)), dma((m - 1, n)), dma((m - 1, n)), dma((n + 1,)),
        ],
        compiler_params=pltpu.CompilerParams(collective_id=0, has_side_effects=True),
        name="gather_records",
    )(records)


def flip(a, bit):
    return a + bit - 2 * bit * lax.rem(a // bit, 2)


def swap(value, axis, bit):
    return lax.ppermute(value, axis, [(i, i ^ bit) for i in range(lax.axis_size(axis))])


def add_up(value, axis):
    for bit in (1, 2):
        value = value + swap(value, axis, bit)
    return value


def iterate(x, kept, n, m):
    total, width = x.shape
    rows = total // n
    r, s = lax.axis_index("rec"), lax.axis_index("smp")
    x = x.reshape(m, rows, width)

    def strip_of(at):
        return lax.dynamic_index_in_dim(x, at, 0, keepdims=False)

    s1, s2 = flip(s, 1), flip(s, 2)
    far = strip_of(s2) + swap(strip_of(flip(s2, 1)), "smp", 1)
    near = strip_of(s) + swap(strip_of(s1), "smp", 1)
    strip = near + swap(far, "smp", 2)
    gram = strip[:, :rows].T / total
    start = add_up(strip[:, rows:], "rec")
    own = add_up(jnp.dot(gram, start, precision=HIGHEST), "smp")
    others = [swap(own, "rec", bit) for bit in (1, 2, 3)]
    second = jnp.zeros((n, rows, kept), jnp.float32)
    for at, value in zip((r, flip(r, 1), flip(r, 2), flip(flip(r, 2), 1)), [own] + others):
        second = lax.dynamic_update_index_in_dim(second, value, at, 0)
    here = lax.dynamic_index_in_dim(second, s, 0, keepdims=False)
    amplitude = add_up(jnp.dot(gram, here, precision=HIGHEST), "smp")
    inner = add_up(jnp.dot(own.T, amplitude, precision=HIGHEST) / total, "rec")
    return second.reshape(total, kept), amplitude, inner


def panel_kernel(total, left_ref, right_ref, *rest):
    out_ref, turned = rest[-2:]

    @pl.when(pl.program_id(0) == 0)
    def _():
        turned[...] = left_ref[...].T

    out_ref[...] = (
        jnp.dot(turned[...], right_ref[...], preferred_element_type=jnp.float32) * (1.0 / total)
    )


def covariance_panel(row_block, block, tile, at, height):
    total, width = block.shape
    across = 512
    in_specs = [
        pl.BlockSpec((total, height), lambda j: (0, at)),
        pl.BlockSpec((total, across), lambda j: (0, j)),
    ]
    args = [row_block, block]
    if tile is not None:
        in_specs.append(pl.BlockSpec(memory_space=pl.ANY))
        args.append(tile)
    return pl.pallas_call(
        functools.partial(panel_kernel, total),
        out_shape=jax.ShapeDtypeStruct((row_block.shape[1], width), jnp.float32),
        grid=(width // across,),
        in_specs=in_specs,
        out_specs=pl.BlockSpec((height, across), lambda j: (at, j)),
        scratch_shapes=[pltpu.VMEM((height, total), jnp.bfloat16)],
        input_output_aliases={} if tile is None else {2: 0},
        compiler_params=pltpu.CompilerParams(vmem_limit_bytes=32 * 2**20),
        cost_estimate=pl.CostEstimate(
            flops=2 * total * height * width,
            bytes_accessed=4 * height * width + 2 * total * (height + width),
            transcendentals=0,
        ),
        name="covariance_panel",
    )(*args)


def pieces(block):
    parts = []
    for _ in range(2):
        high = lax.reduce_precision(block, 8, 7)
        parts.append(high.astype(jnp.bfloat16))
        block = block - high
    parts.append(block.astype(jnp.bfloat16))
    return jnp.concatenate(parts, axis=1)


def exact_dot(left, block, contract):
    kept = block.shape[1]
    out = lax.dot_general(
        left, pieces(block), (((contract,), (0,)), ((), ())), preferred_element_type=jnp.float32
    )
    return out[:, :kept] + out[:, kept : 2 * kept] + out[:, 2 * kept :]


def on_device(records, start_modes):
    rec_dev, width = records.shape
    panels = lax.axis_size("smp")
    total = rec_dev * lax.axis_size("rec")
    sub_width, kept = start_modes.shape[1:]
    full_width = width * panels
    at = lax.axis_index("rec")

    n, m = lax.axis_size("rec"), panels
    direct = n == 4 and m == 4 and sub_width % 256 == 0 and width % 512 == 0 and rec_dev % 128 == 0
    direct = direct and kept % 128 == 0
    if direct:
        block, row_block = gather(records, n, m)
    else:
        block = lax.all_gather(records, "rec", axis=0, tiled=True)
    own = lax.dynamic_slice_in_dim(block, at * sub_width, sub_width, axis=1)
    if not direct:
        row_block = lax.all_gather(own, "smp", axis=1, tiled=True)

    gram_part = lax.dot_general(
        block, records, (((1,), (1,)), ((), ())), preferred_element_type=jnp.float32
    )
    first_part = exact_dot(own, start_modes[0], 1)
    if direct:
        stacked = jnp.concatenate([gram_part, first_part], axis=1)
        second, amplitude, inner = iterate(stacked, kept, n, m)
    else:
        gram = lax.psum(gram_part, "smp").T / total
        first = lax.psum(first_part, ("rec", "smp"))
        second_own = jnp.dot(gram, first, precision=HIGHEST)
        second = lax.all_gather(second_own, "rec", axis=0, tiled=True)
        amplitude = jnp.dot(gram, second, precision=HIGHEST)
        inner = lax.psum(jnp.dot(second_own.T, amplitude, precision=HIGHEST), "rec") / total

    if direct:
        tile = None
        height = sub_width // 2
        for piece in range(2 * panels):
            tile = covariance_panel(row_block, block, tile, piece, height)
    else:
        tile = (
            lax.dot_general(
                row_block, block, (((0,), (0,)), ((), ())), preferred_element_type=jnp.float32
            )
            / total
        )
    covariance = tile.reshape(panels, sub_width, width)

    factor = jnp.linalg.cholesky(inner)
    solved = lax.linalg.triangular_solve(
        factor,
        jnp.concatenate([second, amplitude], axis=0),
        left_side=False,
        lower=True,
        transpose_a=True,
    )
    modes = exact_dot(own, solved[:total], 0) * (math.sqrt(full_width) / total)
    projections = solved[total:] / math.sqrt(full_width)
    return (covariance, modes.reshape(1, sub_width, kept), projections)


def solution(mesh):
    in_specs = (P(("grp", "rec"), "smp"), P("smp", ("grp", "rec"), None))
    out_specs = (
        P(None, ("grp", "rec"), "smp"),
        P("smp", ("grp", "rec"), None),
        P(("grp", "rec"), None),
    )
    return jax.shard_map(
        on_device, mesh=mesh, in_specs=in_specs, out_specs=out_specs, check_vma=False
    )
```
